32 devices in a mesh: req: 8 (over y, x, core), tp: 4 (over z).
Axes of the slice: x: 2, y: 2, z: 4, core: 2. Of those that a mesh axis runs over, the one named last changes fastest.
Arguments:
- activations: bfloat16 [2048, 2304], P('req'), may hold values from -6 to 6
- lengths: int32 [8, 4], P('req'), may hold values from 1 to 192, 256 in all within a row
- adapter_of: int32 [8, 4], P('req'), may hold values from 0 to 15
- slot_of: int32 [16], replicated, may hold values from 0 to 15, as said below
- page_table: int32 [8, 6], P('req'), may hold values from 0 to 5, each once within a row
- experts_of: int32 [2048, 2], P('req'), may hold values from 0 to 7, all different within a row; in each aligned block of 256 rows (0 to 255, 256 to 511, ...) at most 72 rows name the same one
- attn_gain: float32 [2304], replicated, may hold values from 0.25 to 1.75
- moe_gain: float32 [2304], replicated, may hold values from 0.25 to 1.75
- w_qkv: bfloat16 [2304, 3, 2304], P(None, None, 'tp'), may hold values from -4 to 4
- output_weight: bfloat16 [2304, 2304], P('tp'), may hold values from -0.125 to 0.125
- router: bfloat16 [2304, 8], replicated, may hold values from -0.125 to 0.125
- w_gate_up: bfloat16 [8, 2304, 2, 5760], P('req', None, None, 'tp'), may hold values from -0.125 to 0.125
- w_down: bfloat16 [8, 5760, 2304], P('req', 'tp'), may hold values from -0.078125 to 0.078125
- expert_up_factors: bfloat16 [8, 256, 2, 5760], P('req', None, None, 'tp'), may hold values from -0.59765625 to 0.59765625
- pool_a: bfloat16 [16, 2304, 64], P('req'), may hold values from -0.125 to 0.125
- slot_query_key_value_up: bfloat16 [16, 16, 3, 2304], P('req', None, None, 'tp'), may hold values from -0.59765625 to 0.59765625
- pool_aout: bfloat16 [16, 2304, 16], P('req', 'tp'), may hold values from -0.125 to 0.125
- pool_bout: bfloat16 [16, 16, 2304], P('req'), may hold values from -1.796875 to 1.796875
Outputs:
- layer_out: bfloat16 [2048, 2304], P('req')
- page_cache: bfloat16 [48, 128, 2, 2304], P('req', None, None, 'tp')
The draws below stay inside these ranges and needn't reach their ends.
Inputs may be any that keep to these rules, and one draw needn't show every extreme that they name: `slot_of`: distinct slots. `page_table`: each row holds every page index once. `experts_of`: the two experts of a token differ; among the 256 tokens of one index of req at most 72 choose one expert, and some expert reaches 72.
All inputs are finite; a program needn't handle non-finite values.
Results may differ from the reference program's by a relative error of at most 0.0095.
Values may be sent and summed in bfloat16 or wider, within the bound.
A program may use at most 128 MiB of HBM per device.

```python
import math
import jax
import jax.numpy as jnp
import numpy as np
from jax import lax

D = 2304
HEAD_TOTAL = 36
HEAD_SIZE = 64
HD = 2304
EXPERT_UNITS = 5760
EXPERTS = 8
ADAPTER_RANK = 16
ADAPTER_TOTAL = 16
PAGE = 128
REQ_DEV = 4
TOK_DEV = 256
MOST = 192
CAP = 72
TOKENS = 2048
UNIT_SLICES = 1
FFS = 5760
FFT = 1440
SLOTS = 16
POOL_DEV = 6
N_REQ = 8
N_TP = 4


def draw_slot_of(key, part):
    return jax.random.permutation(key, SLOTS)[:ADAPTER_TOTAL].astype(jnp.int32)


def draw_w_qkv(key, part):
    key_base = jax.random.fold_in(key, 0)
    drawn = jnp.clip(jax.random.normal(key_base, (D, 3, HEAD_TOTAL * HEAD_SIZE), jnp.float32), -6.0, 6.0) / math.sqrt(D)
    return drawn.astype(jnp.bfloat16)


def place_ends(values, stream_key, low, top_value):
    longest = values.shape.index(max(values.shape))
    spots = []
    for shift in (0, 1):
        where = [jax.random.randint(jax.random.fold_in(stream_key, axis), (), 0, length) for axis, length in enumerate(values.shape)]
        where[longest] = (where[longest] + shift) % values.shape[longest]
        spots.append(tuple(where))
    return values.at[spots[0]].set(low).at[spots[1]].set(top_value)


def steps_of(own_key, shape, shards, smallest, high):
    def one(axis_at, blocks):
        heights = jax.random.uniform(jax.random.fold_in(jax.random.fold_in(own_key, 6), axis_at), (blocks,), jnp.float32, smallest / len(shards), high / len(shards))
        return jnp.repeat(jnp.exp(heights), shape[axis_at] // blocks).reshape((-1,) + (1,) * (len(shape) - axis_at - 1))

    factor_of = one(*shards[0])
    for cut in shards[1:]:
        factor_of = factor_of * one(*cut)
    return factor_of


def split_up(count, total, reach, slope):
    weights = [(1 << 20) // math.isqrt(rank ** slope) + 1 for rank in range(2, count + 1)]
    spare, given = total - reach - (count - 1), [1] * (count - 1)
    while spare > 0:
        candidates = [i for i in range(count - 1) if given[i] < reach]
        whole, budget = sum([weights[i] for i in candidates]), spare
        for i in candidates:
            more = min(reach - given[i], max(1, budget * weights[i] // whole), spare)
            given[i] = given[i] + more
            spare = spare - more
    return np.array([reach] + given)


def ragged_sizes(rng, count, total, reach, skew):
    if count == 2:
        one = jax.random.randint(rng, (), max(1, total - reach), min(reach, total - 1) + 1)
        return jnp.stack([one, total - one])
    tallies = jnp.asarray(split_up(count, total, reach, skew), jnp.int32)
    couples = (count - 1) // 2
    donor, sink = tallies[1:1 + 2 * couples:2], tallies[2:2 + 2 * couples:2]
    room = jnp.minimum(donor - 1, reach - sink)
    shifted = jax.random.randint(jax.random.fold_in(rng, 1), (couples,), 0, 1 << 20) % (room + 1)
    tallies = tallies.at[1:1 + 2 * couples:2].set(donor - shifted).at[2:2 + 2 * couples:2].set(sink + shifted)
    return tallies[jax.random.permutation(jax.random.fold_in(rng, 2), count)]


def assign_block(rng, own, number, rows, count, top, bound, lean):
    sequence = jax.random.permutation(rng, count)
    crowded, ordinary = portions_of(count, rows * top, bound, lean, True), portions_of(count, rows * top, bound, lean, False)
    places = jnp.arange(count)

    def named(sizes, turn):
        used = int((sizes > 0).sum())
        fixed = max(1, used // 4)
        passed = fixed + (places - fixed + turn * (used - fixed)) % max(1, count - fixed)
        return jnp.zeros((count,), jnp.int32).at[sequence[jnp.where(places < fixed, places, passed)]].set(jnp.asarray(sizes, jnp.int32))

    sizes = jnp.where(number % 4 == 0, named(crowded, number // 4), named(ordinary, number - number // 4 - 1))
    mixed = jax.random.permutation(jax.random.fold_in(own, 3), count)
    source_of, sink = mixed[0:count // 2 * 2:2], mixed[1:count // 2 * 2:2]
    slack = jnp.minimum(sizes[source_of] - 1, bound - sizes[sink]) // 2
    slack = jnp.where((source_of == sequence[0]) | (sink == sequence[0]) | (sizes[sink] == 0), 0, jnp.maximum(slack, 0))
    passed = jax.random.randint(jax.random.fold_in(own, 4), (count // 2,), 0, 1 << 20) % (slack + 1)
    sizes = sizes.at[source_of].add(-passed).at[sink].add(passed)
    items = jnp.searchsorted(jnp.cumsum(sizes), jnp.arange(rows * top), side="right").astype(jnp.int32)
    grid = items.reshape(top, rows).T
    grid = grid[jax.random.permutation(jax.random.fold_in(own, 1), rows)]
    turn = jax.random.randint(jax.random.fold_in(own, 2), (rows, 1), 0, top)
    return jnp.take_along_axis(grid, (jnp.arange(top)[None, :] + turn) % top, axis=1)


def portions_of(number_of, total, bound, lean, full):
    loads = [(1 << 20) // math.isqrt(rank ** lean) + 1 for rank in range(1, number_of + 1)]
    largest = bound if full else min(bound, max(-(-total // number_of), total * loads[0] // sum(loads)))
    least = 1 if total - largest >= number_of - 1 else 0
    counts, surplus = [largest] + [least] * (number_of - 1), total - largest - least * (number_of - 1)
    while surplus > 0:
        free = [i for i in range(1, number_of) if counts[i] < largest] or [i for i in range(1, number_of) if counts[i] < bound]
        pool, left = sum([loads[i] for i in free]), surplus
        for i in free:
            more = min(bound - counts[i], max(1, left * loads[i] // pool), surplus)
            counts[i] = counts[i] + more
            surplus = surplus - more
    return np.array(counts)


def normal_values(rng, extent, scale, bound, shards=(), kind=jnp.bfloat16):
    values = jax.random.normal(rng, extent, jnp.float32) * scale
    if len(shards) > 0:
        values = steps_of(rng, extent, shards, -0.22, 0.18) * values
    return jnp.clip(values, min=-bound, max=bound).astype(kind)


def setup_inputs(seed: int = 0) -> dict:
    splits = jax.random.split(jax.random.key(seed), 19)
    activations = normal_values(splits[0], (TOKENS, D), 1.0, 6.0, ((0, 8),))
    lengths = jax.vmap(lambda own: ragged_sizes(own, REQ_DEV, TOK_DEV, MOST, 2))(jax.random.split(splits[1], N_REQ)).reshape((N_REQ, REQ_DEV)).astype(jnp.int32)
    adapter_of = place_ends(jax.random.randint(splits[2], (N_REQ, REQ_DEV), 0, ADAPTER_TOTAL), jax.random.fold_in(splits[2], 1), 0, ADAPTER_TOTAL - 1).astype(jnp.int32)
    slot_of = draw_slot_of(jax.random.fold_in(splits[18], 71), 0)
    page_table = jax.vmap(lambda own: jax.random.permutation(own, POOL_DEV))(jax.random.split(splits[4], N_REQ)).reshape((N_REQ, POOL_DEV)).astype(jnp.int32)
    experts_of_keys = jax.random.split(jax.random.fold_in(splits[5], 1), TOKENS // TOK_DEV)
    experts_of_turns = jax.random.permutation(jax.random.fold_in(splits[5], 3), TOKENS // TOK_DEV)
    experts_of = jax.vmap(lambda own, number: assign_block(jax.random.fold_in(splits[5], 2), own, number, TOK_DEV, EXPERTS, 2, CAP, 2))(experts_of_keys, experts_of_turns).reshape((TOKENS, 2))
    attn_gain = jnp.clip(1.0 + 0.15 * jax.random.normal(splits[6], (D,), jnp.float32), 0.25, 1.75)
    moe_gain = jnp.clip(1.0 + 0.15 * jax.random.normal(splits[7], (D,), jnp.float32), 0.25, 1.75)
    w_qkv = draw_w_qkv(jax.random.fold_in(splits[18], 71), 0)
    output_weight = normal_values(splits[9], (HD, D), HD ** -0.5, 0.125, ((0, 4),))
    router = normal_values(splits[10], (D, EXPERTS), D ** -0.5, 0.125)
    w_gate_up = normal_values(splits[11], (N_REQ, D, 2, FFS), D ** -0.5, 0.125, ((0, 8), (3, 4)))
    w_down = normal_values(splits[12], (N_REQ, FFS, D), EXPERT_UNITS ** -0.5, 0.078125, ((0, 8), (1, 4)))
    expert_up_factors = normal_values(splits[13], (N_REQ, ADAPTER_TOTAL * ADAPTER_RANK, 2, FFS), 0.1, 0.59765625, ((0, 8), (3, 4)))
    pool_a = normal_values(splits[14], (SLOTS, D, 4 * ADAPTER_RANK), D ** -0.5, 0.125, ((0, 8),))
    slot_query_key_value_up = normal_values(splits[15], (SLOTS, ADAPTER_RANK, 3, HD), 0.1, 0.59765625, ((0, 8), (3, 4)))
    pool_aout = normal_values(splits[16], (SLOTS, HD, ADAPTER_RANK), HD ** -0.5, 0.125, ((0, 8), (1, 4)))
    pool_bout = normal_values(splits[17], (SLOTS, ADAPTER_RANK, D), 0.3, 1.796875, ((0, 8),))
    return {"activations": activations, "lengths": lengths, "adapter_of": adapter_of, "slot_of": slot_of, "page_table": page_table, "experts_of": experts_of, "attn_gain": attn_gain, "moe_gain": moe_gain, "w_qkv": w_qkv, "output_weight": output_weight, "router": router, "w_gate_up": w_gate_up, "w_down": w_down, "expert_up_factors": expert_up_factors, "pool_a": pool_a, "slot_query_key_value_up": slot_query_key_value_up, "pool_aout": pool_aout, "pool_bout": pool_bout}


epsilon = 1e-05
adapter_scale = 2.0
rope_base = 10000.0

def rms_norm(values, scales):
    mean_sq = lax.optimization_barrier(jnp.mean(values * values, axis=-1, keepdims=True))
    return values * lax.rsqrt(mean_sq + epsilon) * scales

def token_layout(lengths_row, tok_count):
    ends_at = jnp.cumsum(lengths_row)
    starts = ends_at - lengths_row
    places = jnp.arange(tok_count, dtype=jnp.int32)
    request = lax.optimization_barrier(jnp.sum((places[:, None] >= ends_at[None, :]).astype(jnp.int32), axis=1))
    position = places - starts[request]
    return (request.astype(jnp.int32), position.astype(jnp.int32))

def rotate(values, position):
    head_dim = values.shape[-1]
    half_dim = head_dim // 2
    frequency = rope_base ** (-jnp.arange(half_dim, dtype=jnp.float32) * 2.0 / head_dim)
    angles = position.astype(jnp.float32)[:, None] * frequency[None, :]
    cosine = jnp.cos(angles)[:, None, :]
    sine_part = jnp.sin(angles)[:, None, :]
    front_half = values[..., :half_dim]
    back_half = values[..., half_dim:]
    return jnp.concatenate([front_half * cosine - back_half * sine_part, back_half * cosine + front_half * sine_part], axis=-1)

def attend(queries, keys_roped, values, request, position):
    scores = jnp.einsum('qhd,khd->hqk', queries.astype(jnp.float32), keys_roped.astype(jnp.float32)) * (1.0 / math.sqrt(HEAD_SIZE))
    allowed = (request[:, None] == request[None, :]) & (position[None, :] <= position[:, None])
    scores = jnp.where(allowed[None], scores, -1e+30)
    row_max = lax.optimization_barrier(jnp.max(scores, axis=-1, keepdims=True))
    weights = jnp.exp(scores - row_max)
    weights = (weights / lax.optimization_barrier(jnp.sum(weights, axis=-1, keepdims=True))).astype(jnp.bfloat16)
    return jnp.einsum('hqk,khd->qhd', weights.astype(jnp.float32), values.astype(jnp.float32)).astype(jnp.bfloat16)

def reference(activations, lengths, adapter_of, slot_of, page_table, experts_of, attn_gain, moe_gain, w_qkv, output_weight, router, w_gate_up, w_down, expert_up_factors, pool_a, slot_query_key_value_up, pool_aout, pool_bout):
    n_req = lengths.shape[0]
    token_share = activations.shape[0] // n_req
    tok_all = activations.shape[0]
    request, position = jax.vmap(lambda row: token_layout(row, token_share))(lengths)
    request = request.reshape(-1)
    position = position.reshape(-1)
    device = jnp.arange(tok_all, dtype=jnp.int32) // token_share
    adapter = adapter_of[device, request]
    token_slot = slot_of[adapter]
    slot_count = pool_a.shape[0]
    slot_hot = token_slot[:, None] == jnp.arange(slot_count, dtype=jnp.int32)[None, :]
    normed = rms_norm(activations.astype(jnp.float32), attn_gain).astype(jnp.bfloat16)
    factor_qkv = pool_a[:, :, :3 * ADAPTER_RANK].transpose(1, 0, 2).reshape(D, slot_count * 3 * ADAPTER_RANK)
    down_all = jnp.dot(normed, factor_qkv, preferred_element_type=jnp.float32).reshape(-1, slot_count, 3, ADAPTER_RANK)
    coeff_qkv = lax.optimization_barrier(jnp.sum(jnp.where(slot_hot[:, :, None, None], down_all, 0.0), axis=1)).astype(jnp.bfloat16)
    spread_rows = jnp.where(slot_hot[:, :, None, None], coeff_qkv.astype(jnp.float32)[:, None], 0.0)
    adapter_query_key_value = jnp.einsum('qwxv,wvxd->qxd', spread_rows, slot_query_key_value_up.astype(jnp.float32))
    plain_query_key_value = jnp.dot(normed, w_qkv.reshape(D, 3 * HD), preferred_element_type=jnp.float32).reshape(-1, 3, HD)
    projection_result = (plain_query_key_value + adapter_scale * adapter_query_key_value).reshape(-1, 3, HEAD_TOTAL, HEAD_SIZE)
    queries = rotate(projection_result[:, 0], position).astype(jnp.bfloat16)
    keys_roped = rotate(projection_result[:, 1], position).astype(jnp.bfloat16)
    values = projection_result[:, 2].astype(jnp.bfloat16)
    pages_used = (lengths + PAGE - 1) // PAGE
    first_page = jnp.cumsum(pages_used, axis=1) - pages_used
    pool_dev = page_table.shape[1]
    local_page = page_table[device, first_page[device, request] + position // PAGE]
    cache_row = (device * pool_dev + local_page) * PAGE + position % PAGE
    key_value = jnp.stack([keys_roped.reshape(-1, HD), values.reshape(-1, HD)], axis=1)
    page_cache = jnp.zeros((n_req * pool_dev * PAGE, 2, HD), jnp.bfloat16).at[cache_row].set(key_value)
    page_cache = page_cache.reshape(n_req * pool_dev, PAGE, 2, HD)

    def one_device(pieces):
        return attend(pieces[0], pieces[1], pieces[2], pieces[3], pieces[4])
    attention_result = lax.map(one_device, (queries.reshape(n_req, token_share, HEAD_TOTAL, HEAD_SIZE), keys_roped.reshape(n_req, token_share, HEAD_TOTAL, HEAD_SIZE), values.reshape(n_req, token_share, HEAD_TOTAL, HEAD_SIZE), request.reshape(n_req, token_share), position.reshape(n_req, token_share))).reshape(-1, HD)
    aout_all = jnp.dot(attention_result, pool_aout.transpose(1, 0, 2).reshape(HD, slot_count * ADAPTER_RANK), preferred_element_type=jnp.float32).reshape(-1, slot_count, ADAPTER_RANK)
    coeff_out = lax.optimization_barrier(jnp.sum(jnp.where(slot_hot[:, :, None], aout_all, 0.0), axis=1))
    spread_out = jnp.where(slot_hot[:, :, None], coeff_out[:, None, :], 0.0).reshape(-1, slot_count * ADAPTER_RANK)
    output_update = jnp.dot(spread_out, pool_bout.astype(jnp.float32).reshape(slot_count * ADAPTER_RANK, D), precision=lax.Precision.HIGHEST)
    residual_stream = activations.astype(jnp.float32) + (jnp.dot(attention_result, output_weight, preferred_element_type=jnp.float32) + adapter_scale * output_update)
    normed_moe = rms_norm(residual_stream, moe_gain).astype(jnp.bfloat16)
    logits = jnp.dot(normed_moe, router, preferred_element_type=jnp.float32)
    chosen = jnp.take_along_axis(logits, experts_of, axis=1)
    gate_weights = 1.0 / (1.0 + jnp.exp(chosen[:, ::-1] - chosen))
    exp_all = jnp.dot(normed_moe, pool_a[:, :, 3 * ADAPTER_RANK:].transpose(1, 0, 2).reshape(D, slot_count * ADAPTER_RANK), preferred_element_type=jnp.float32).reshape(-1, slot_count, ADAPTER_RANK)
    coeff_exp = lax.optimization_barrier(jnp.sum(jnp.where(slot_hot[:, :, None], exp_all, 0.0), axis=1)).astype(jnp.bfloat16)
    flat_expert = experts_of.reshape(n_req, 2 * token_share)
    expert_hot = (flat_expert[:, :, None] == jnp.arange(EXPERTS, dtype=jnp.int32)[None, None, :]).astype(jnp.int32)
    order_in = lax.optimization_barrier(jnp.sum((jnp.cumsum(expert_hot, axis=1) - expert_hot) * expert_hot, axis=2))
    slot_place = jnp.arange(n_req, dtype=jnp.int32)[:, None] * CAP + order_in
    assign = jnp.arange(2 * tok_all, dtype=jnp.int32).reshape(n_req, 2 * token_share)
    slot_table = jnp.full((EXPERTS, n_req * CAP), 2 * tok_all, jnp.int32).at[flat_expert.reshape(-1), slot_place.reshape(-1)].set(assign.reshape(-1))
    rows_pad = jnp.concatenate([normed_moe, jnp.zeros((1, D), jnp.bfloat16)], axis=0)
    coeff_pad = jnp.concatenate([coeff_exp, jnp.zeros((1, ADAPTER_RANK), jnp.bfloat16)], axis=0)
    adapter_pad = jnp.concatenate([adapter, jnp.zeros((1,), jnp.int32)], axis=0)
    blocks = UNIT_SLICES * N_TP

    def expert_rows(expert_choice):
        members = slot_table[expert_choice] // 2
        expert_input_rows = rows_pad[members]
        coeff_rank = coeff_pad[members]
        adapter_ids = adapter_pad[members]
        gate_up_product = lax.dynamic_slice_in_dim(w_gate_up, expert_choice * UNIT_SLICES, UNIT_SLICES, 0).transpose(1, 2, 0, 3).reshape(D, 2 * EXPERT_UNITS)
        adapter_up_product = lax.dynamic_slice_in_dim(expert_up_factors, expert_choice * UNIT_SLICES, UNIT_SLICES, 0).transpose(1, 2, 0, 3).reshape(ADAPTER_TOTAL * ADAPTER_RANK, 2 * EXPERT_UNITS)
        broad_coefficients = jnp.where(adapter_ids[:, None, None] == jnp.arange(ADAPTER_TOTAL, dtype=jnp.int32)[None, :, None], coeff_rank[:, None, :], jnp.zeros((), jnp.bfloat16)).reshape(-1, ADAPTER_TOTAL * ADAPTER_RANK)
        before_norm = jnp.dot(expert_input_rows, gate_up_product, preferred_element_type=jnp.float32) + adapter_scale * jnp.dot(broad_coefficients, adapter_up_product, preferred_element_type=jnp.float32)
        before_norm = before_norm.reshape(-1, 2, EXPERT_UNITS)
        hidden = (jax.nn.silu(before_norm[:, 0]) * before_norm[:, 1]).astype(jnp.bfloat16)
        down_slice = lax.dynamic_slice_in_dim(w_down, expert_choice * UNIT_SLICES, UNIT_SLICES, 0).reshape(blocks, FFT, D)
        hidden_blocks = hidden.reshape(-1, blocks, FFT)

        def add_block(block_index, running):
            partial_term = jnp.dot(hidden_blocks[:, block_index], down_slice[block_index], preferred_element_type=jnp.float32).astype(jnp.bfloat16)
            partial_term = lax.optimization_barrier(partial_term)
            return running + partial_term.astype(jnp.float32)
        return lax.fori_loop(0, blocks, add_block, jnp.zeros((expert_input_rows.shape[0], D), jnp.float32))
    outputs = lax.map(expert_rows, jnp.arange(EXPERTS, dtype=jnp.int32))
    gathered = outputs[flat_expert.reshape(-1), slot_place.reshape(-1)].reshape(-1, 2, D)
    moe_sum = lax.optimization_barrier(jnp.sum(gate_weights[:, :, None] * gathered, axis=1))
    layer_out = (residual_stream + moe_sum).astype(jnp.bfloat16)
    return (layer_out, page_cache)
```

```python
import math

import jax
import jax.numpy as jnp
import numpy as np
from jax import lax
from jax.sharding import PartitionSpec as P

HEAD_SIZE = 64
EXPERTS = 8
ADAPTER_RANK = 16
PAGE = 128
CAP = 72
PIECES = 2

epsilon = 1e-05
adapter_scale = 2.0
rope_base = 10000.0

BF = jnp.bfloat16
F32 = jnp.float32


def iota(shape, dim):
    return lax.broadcasted_iota(jnp.int32, shape, dim)


def dot(a, b):
    return jnp.dot(a, b, preferred_element_type=F32)


def dot_nt(a, b):
    return lax.dot_general(a, b, (((1,), (1,)), ((), ())), preferred_element_type=F32)


def dot_tn(a, b):
    return lax.dot_general(a, b, (((0,), (0,)), ((), ())), preferred_element_type=F32)


def split_two(x):
    high = lax.reduce_precision(x, 8, 7)
    return high.astype(BF), (x - high).astype(BF)


def rope_tables(count):
    half = HEAD_SIZE // 2
    frequency = np.float32(rope_base) ** (-np.arange(half, dtype=np.float32) * np.float32(2.0) / HEAD_SIZE)
    angles = np.arange(count, dtype=np.float32)[:, None] * frequency[None, :].astype(np.float32)
    table = np.concatenate([np.cos(angles), np.sin(angles)], axis=1).astype(np.float32)
    parts = []
    for _ in range(3):
        part = table.astype(BF)
        parts.append(part)
        table = table - part.astype(np.float32)
    return np.concatenate(parts, axis=0)


def pieces_of(width):
    units = width // 128
    sizes = [(units * (i + 1)) // PIECES - (units * i) // PIECES for i in range(PIECES)]
    sizes[-1] += 0
    cuts, at = [], 0
    for i, size in enumerate(sizes):
        end = width if i == PIECES - 1 else at + size * 128
        cuts.append((at, end))
        at = end
    return cuts


def sum_tp(x, earlier):
    if earlier:
        x, _ = lax.optimization_barrier((x, earlier[-1]))
    return lax.psum(x, "tp")


def per_device(
    activations,
    lengths,
    adapter_of,
    slot_of,
    page_table,
    experts_of,
    attn_gain,
    moe_gain,
    w_qkv,
    output_weight,
    router,
    w_gate_up,
    w_down,
    expert_up_factors,
    pool_a,
    slot_query_key_value_up,
    pool_aout,
    pool_bout,
):
    T, D = activations.shape
    n_req = lax.axis_size("req")
    n_tp = lax.axis_size("tp")
    R = ADAPTER_RANK
    width = w_qkv.shape[2]
    heads = width // HEAD_SIZE
    own = pool_a.shape[0]
    n_slots = own * n_req
    n_adapters = slot_of.shape[0]
    share = D // n_tp
    pad = -share % 128
    pad_w = -width % 128

    my_tp = lax.axis_index("tp")
    down_t = pool_a.transpose(0, 2, 1)
    down_part = lax.dynamic_slice_in_dim(down_t[:, : 3 * R], my_tp * share, share, 2)
    up_t = slot_query_key_value_up.transpose(0, 2, 1, 3).reshape(own, 3 * R, width)
    aout_t = pool_aout.transpose(0, 2, 1)
    pool_down = lax.all_gather(
        jnp.pad(down_part, ((0, 0), (0, 0), (0, pad))), "req", axis=0, tiled=True
    )[:, :, :share]
    pool_up = lax.all_gather(
        jnp.pad(jnp.concatenate([up_t, aout_t], axis=1), ((0, 0), (0, 0), (0, pad_w))),
        "req",
        axis=0,
        tiled=True,
    )[:, :, :width]
    pool_exp = lax.all_gather(down_t[:, 3 * R :], "req", axis=0, tiled=True)
    pool_bup = lax.all_gather(pool_bout, "req", axis=0, tiled=True)

    row = lengths[0]
    n_in = row.shape[0]
    ends = jnp.sum(jnp.where(iota((n_in, n_in), 0) <= iota((n_in, n_in), 1), row[:, None], 0), axis=0)
    starts = ends - row
    pages = (row + PAGE - 1) // PAGE
    first_page = jnp.sum(
        jnp.where(iota((n_in, n_in), 0) < iota((n_in, n_in), 1), pages[:, None], 0), axis=0
    )
    slots_in = jnp.sum(
        jnp.where(
            adapter_of[0][:, None] == iota((n_in, n_adapters), 1), slot_of[None, :], 0
        ),
        axis=1,
    )
    place = iota((T, n_in), 0)
    here = (place >= starts[None, :]) & (place < ends[None, :])

    def of_request(values):
        return jnp.sum(jnp.where(here, values[None, :], 0), axis=1, keepdims=True)

    start = of_request(starts)
    token_slot = of_request(slots_in)
    adapter = of_request(adapter_of[0])
    position = iota((T, 1), 0) - start
    page_at = of_request(first_page) + position // PAGE
    n_pages = page_table.shape[1]
    local_page = jnp.sum(
        jnp.where(page_at == iota((T, n_pages), 1), page_table, 0), axis=1, keepdims=True
    )
    cache_row = local_page * PAGE + position % PAGE

    def slot_mask(each):
        return token_slot == iota((T, n_slots * each), 1) // each

    mask_r = slot_mask(R)

    act = activations.astype(F32)
    mean_sq = jnp.mean(act * act, axis=-1, keepdims=True)
    normed = (act * lax.rsqrt(mean_sq + epsilon) * attn_gain).astype(BF)
    normed = lax.optimization_barrier(normed)
    plain = [dot_nt(w_qkv[:, p].T, normed) for p in range(3)]
    normed_part = lax.dynamic_slice_in_dim(normed, my_tp * share, share, 1)
    coeff_mask = slot_mask(1)
    down_all = dot_nt(
        pool_down.transpose(1, 0, 2).reshape(3 * R * n_slots, share), normed_part
    ).reshape(3 * R, n_slots, T)
    slot_row = coeff_mask.T
    coeff_part = jnp.sum(jnp.where(slot_row[None], down_all, 0.0), axis=1)
    coeff = lax.psum(coeff_part, "tp").astype(BF)

    projected = []
    for p in range(3):
        spread = jnp.where(
            slot_row[:, None, :],
            coeff[p * R : (p + 1) * R][None] * jnp.array(adapter_scale, BF),
            jnp.zeros((), BF),
        ).reshape(n_slots * R, T)
        up = pool_up[:, p * R : (p + 1) * R].reshape(n_slots * R, width)
        projected.append(plain[p] + dot_tn(up, spread))

    tables = jnp.asarray(rope_tables(T))
    hot = (position == iota((T, T), 1)).astype(BF)
    turned = lax.dot_general(
        tables,
        jnp.concatenate([hot, hot, hot], axis=1),
        (((0,), (1,)), ((), ())),
        preferred_element_type=F32,
    )
    half = HEAD_SIZE // 2
    cosine, sine = turned[None, :half], turned[None, half:]

    def rotate(x):
        x = x.reshape(heads, HEAD_SIZE, T)
        front, back = x[:, :half], x[:, half:]
        return jnp.concatenate(
            [front * cosine - back * sine, back * cosine + front * sine], axis=1
        ).astype(BF)

    queries = rotate(projected[0])
    keys = rotate(projected[1])
    values = projected[2].astype(BF).reshape(heads, HEAD_SIZE, T)

    place_hot = (cache_row == iota((T, n_pages * PAGE), 1)).astype(BF)
    cache = [
        lax.dot_general(
            place_hot, x.reshape(width, T), (((0,), (1,)), ((), ())), preferred_element_type=F32
        )
        .astype(BF)
        .reshape(n_pages, PAGE, width)
        for x in (keys, values)
    ]
    page_cache = jnp.stack(cache, axis=2)

    scores = jnp.einsum("hdq,hdk->hqk", queries, keys, preferred_element_type=F32) * (
        1.0 / math.sqrt(HEAD_SIZE)
    )
    seen = iota((T, T), 1)
    allowed = (seen <= iota((T, T), 0)) & (seen >= start)
    scores = jnp.where(allowed[None], scores, -1e30)
    weights = jnp.exp(scores - jnp.max(scores, axis=-1, keepdims=True))
    weights = (weights / jnp.sum(weights, axis=-1, keepdims=True)).astype(BF)
    attended = (
        jnp.einsum("hqk,hdk->qhd", weights, values, preferred_element_type=F32)
        .astype(BF)
        .reshape(T, width)
    )

    aout_all = dot_nt(attended, pool_up[:, 3 * R :].reshape(n_slots * R, width))
    spread_hi, spread_lo = split_two(jnp.where(mask_r, adapter_scale * aout_all, 0.0))
    cuts = pieces_of(D)
    bup = pool_bup.reshape(n_slots * R, D)
    mixed = []
    for at, end in cuts:
        term = (
            dot(attended, output_weight[:, at:end])
            + dot(spread_hi, bup[:, at:end])
            + dot(spread_lo, bup[:, at:end])
        )
        mixed.append(sum_tp(term.astype(BF), mixed))

    split = n_req // EXPERTS
    experts = [experts_of[:, k : k + 1] for k in range(2)]
    hots = [e == iota((T, EXPERTS), 1) for e in experts]
    chosen_any = (hots[0] | hots[1]).astype(BF)
    before = (iota((T, T), 1) < iota((T, T), 0)).astype(BF)
    prior = dot(before, chosen_any).astype(jnp.int32)
    picks = []
    for k in range(2):
        order = jnp.sum(jnp.where(hots[k], prior, 0), axis=1, keepdims=True)
        picks.append(experts[k] * CAP + order == iota((T, EXPERTS * CAP), 1))
    route = (picks[0] | picks[1]).astype(BF)

    def send(x):
        rows = dot_tn(route, x).astype(BF).reshape(EXPERTS, 1, CAP, x.shape[1])
        rows = jnp.broadcast_to(rows, (EXPERTS, split, CAP, x.shape[1]))
        got = lax.all_to_all(
            rows.reshape(n_req, CAP, x.shape[1]), "req", split_axis=0, concat_axis=0, tiled=True
        )
        return got.reshape(n_req * CAP, x.shape[1])

    units = w_gate_up.shape[3]
    residual = []
    pre = []
    before_act = None
    square = 0.0
    for (at, end), mix in zip(cuts, mixed):
        res = act[:, at:end] + mix.astype(F32)
        residual.append(res)
        square = square + jnp.sum(res * res, axis=-1, keepdims=True)
        pre_p = (res * moe_gain[None, at:end]).astype(BF)
        pre.append(pre_p)
        rows = send(pre_p)
        gu = w_gate_up[0, at:end].reshape(end - at, 2 * units)
        part = dot(rows, gu)
        before_act = part if before_act is None else before_act + part
    scale = lax.rsqrt(square / D + epsilon)
    exp_all = 0.0
    logits = 0.0
    pool_exp = pool_exp.reshape(n_slots * R, D)
    for (at, end), pre_p in zip(cuts, pre):
        exp_all = exp_all + dot_nt(pre_p, pool_exp[:, at:end])
        logits = logits + dot(pre_p, router[at:end])
    logits = logits * scale
    coeff_exp = jnp.where(mask_r, exp_all * scale, 0.0).astype(BF)
    fold = (iota((n_slots * R, R), 0) % R == iota((n_slots * R, R), 1)).astype(BF)
    coeff_exp = dot(coeff_exp, fold).astype(BF)
    scale_hi, scale_lo = split_two(scale)
    meta = jnp.concatenate([coeff_exp, adapter.astype(BF), scale_hi, scale_lo], axis=1)
    got = send(meta)
    got_coeff = got[:, :R]
    got_ids = got[:, R : R + 1].astype(jnp.int32)
    got_scale = got[:, R + 1 : R + 2].astype(F32) + got[:, R + 2 : R + 3].astype(F32)
    unfold = (iota((R, n_adapters * R), 1) % R == iota((R, n_adapters * R), 0)).astype(BF)
    broad = dot(got_coeff * jnp.array(adapter_scale, BF), unfold)
    broad = jnp.where(
        got_ids == iota((n_req * CAP, n_adapters * R), 1) // R, broad, 0.0
    ).astype(BF)
    before_act = before_act * got_scale + dot(
        broad, expert_up_factors[0].reshape(n_adapters * R, 2 * units)
    )
    hidden = (jax.nn.silu(before_act[:, :units]) * before_act[:, units:]).astype(BF)

    chosen = [
        jnp.sum(jnp.where(hots[k], logits, 0.0), axis=1, keepdims=True) for k in range(2)
    ]
    gates = [1.0 / (1.0 + jnp.exp(chosen[1 - k] - chosen[k])) for k in range(2)]
    combine = jnp.where(picks[0], gates[0], 0.0) + jnp.where(picks[1], gates[1], 0.0)
    combine = jnp.broadcast_to(
        combine.reshape(T, EXPERTS, 1, CAP), (T, EXPERTS, split, CAP)
    ).reshape(T, n_req * CAP)
    combine_hi, combine_lo = split_two(combine)

    outs, moe_sums = [], []
    for (at, end), res in zip(cuts, residual):
        part = dot(hidden, w_down[0][:, at:end]).astype(BF)
        back = lax.all_to_all(
            part.reshape(n_req, CAP, end - at), "req", split_axis=0, concat_axis=0, tiled=True
        ).reshape(n_req * CAP, end - at)
        moe = dot(combine_hi, back) + dot(combine_lo, back)
        moe_sums.append(sum_tp(moe.astype(BF), moe_sums))
        outs.append((res + moe_sums[-1].astype(F32)).astype(BF))
    layer_out = jnp.concatenate(outs, axis=1)
    return (layer_out, page_cache)


def solution(mesh):
    return jax.shard_map(
        per_device,
        mesh=mesh,
        in_specs=(
            P("req", None),
            P("req", None),
            P("req", None),
            P(),
            P("req", None),
            P("req", None),
            P(),
            P(),
            P(None, None, "tp"),
            P("tp", None),
            P(),
            P("req", None, None, "tp"),
            P("req", "tp", None),
            P("req", None, None, "tp"),
            P("req", None, None),
            P("req", None, None, "tp"),
            P("req", "tp", None),
            P("req", None, None),
        ),
        out_specs=(P("req", None), P("req", None, None, "tp")),
        check_vma=False,
    )
```

```python
import functools
import math

import jax
import jax.numpy as jnp
import numpy as np
from jax import lax
from jax.experimental import pallas as pl
from jax.experimental.pallas import tpu as pltpu
from jax.sharding import PartitionSpec as P

HEAD_SIZE = 64
EXPERTS = 8
ADAPTER_RANK = 16
PAGE = 128
CAP = 72
PIECES = 3
MESH = pl.DeviceIdType.MESH
VMEM_BYTES = 44 * 2**20

epsilon = 1e-05
adapter_scale = 2.0
rope_base = 10000.0

BF = jnp.bfloat16
F32 = jnp.float32


def iota(shape, dim):
    return lax.broadcasted_iota(jnp.int32, shape, dim)


def dot(a, b):
    return jnp.dot(a, b, preferred_element_type=F32)


def dot_nt(a, b):
    return lax.dot_general(a, b, (((1,), (1,)), ((), ())), preferred_element_type=F32)


def dot_tn(a, b):
    return lax.dot_general(a, b, (((0,), (0,)), ((), ())), preferred_element_type=F32)


def split_two(x):
    high = lax.reduce_precision(x, 8, 7)
    return high.astype(BF), (x - high).astype(BF)


def rope_tables(count):
    half = HEAD_SIZE // 2
    frequency = np.float32(rope_base) ** (-np.arange(half, dtype=np.float32) * np.float32(2.0) / HEAD_SIZE)
    angles = np.arange(count, dtype=np.float32)[:, None] * frequency[None, :].astype(np.float32)
    table = np.concatenate([np.cos(angles), np.sin(angles)], axis=1).astype(np.float32)
    parts = []
    for _ in range(3):
        part = table.astype(BF)
        parts.append(part)
        table = table - part.astype(np.float32)
    return np.concatenate(parts, axis=0)


def pieces_of(width):
    units = width // 128
    sizes = [(units * (i + 1)) // PIECES - (units * i) // PIECES for i in range(PIECES)]
    sizes[-1] += 0
    cuts, at = [], 0
    for i, size in enumerate(sizes):
        end = width if i == PIECES - 1 else at + size * 128
        cuts.append((at, end))
        at = end
    return cuts


def greet(tp_too, req_too, n_tp, n_req):
    barrier = pltpu.get_barrier_semaphore()
    count = 0
    for axis, n, wanted in (("tp", n_tp, tp_too), ("req", n_req, req_too)):
        if wanted:
            me = lax.axis_index(axis)
            for k in range(1, n):
                pl.semaphore_signal(
                    barrier, inc=1, device_id={axis: lax.rem(me + k, n)}, device_id_type=MESH
                )
            count += n - 1
    pl.semaphore_wait(barrier, count)


def remote(src, dst, send_sem, recv_sem, axis, peer):
    return pltpu.make_async_remote_copy(
        src_ref=src,
        dst_ref=dst,
        send_sem=send_sem,
        recv_sem=recv_sem,
        device_id={axis: peer},
        device_id_type=MESH,
    )


def small_sum_kernel(n_tp, x_ref, o_ref, buf, send, recv):
    me = lax.axis_index("tp")
    greet(True, False, n_tp, 1)
    copies = []
    for k in range(1, n_tp):
        c = remote(x_ref, buf.at[k - 1], send.at[k], recv.at[k], "tp", lax.rem(me + k, n_tp))
        c.start()
        copies.append(c)
    total = x_ref[...]
    for c in copies:
        c.wait_recv()
    for k in range(1, n_tp):
        total = total + buf[k - 1]
    o_ref[...] = total
    for c in copies:
        c.wait_send()


def small_sum(x, n_tp):
    return pl.pallas_call(
        functools.partial(small_sum_kernel, n_tp),
        out_shape=jax.ShapeDtypeStruct(x.shape, x.dtype),
        in_specs=[pl.BlockSpec(memory_space=pltpu.VMEM)],
        out_specs=pl.BlockSpec(memory_space=pltpu.VMEM),
        scratch_shapes=[
            pltpu.VMEM((n_tp - 1,) + x.shape, x.dtype),
            pltpu.SemaphoreType.DMA((n_tp,)),
            pltpu.SemaphoreType.DMA((n_tp,)),
        ],
        compiler_params=pltpu.CompilerParams(
            collective_id=0, has_side_effects=True, vmem_limit_bytes=VMEM_BYTES
        ),
    )(x)


def dispatch_kernel(
    n_tp, n_req, term, act, gain, route, rows, normed, res, rs_buf, out_buf,
    rs_send, rs_recv, ag_send, ag_recv, a2a_send, a2a_recv,
):
    my, me = lax.axis_index("tp"), lax.axis_index("req")
    chunk, D = act.shape
    split = n_req // EXPERTS
    greet(True, True, n_tp, n_req)
    copies = []
    for k in range(1, n_tp):
        peer = lax.rem(my + k, n_tp)
        c = remote(term.at[peer], rs_buf.at[k - 1], rs_send.at[k], rs_recv.at[k], "tp", peer)
        c.start()
        copies.append(c)
    total = act[...].astype(F32) + term[my].astype(F32)
    for k in range(1, n_tp):
        copies[k - 1].wait_recv()
        total = total + rs_buf[k - 1].astype(F32)
    res[...] = total
    mean_sq = jnp.mean(total * total, axis=-1, keepdims=True)
    normed[my] = (total * lax.rsqrt(mean_sq + epsilon) * gain[...]).astype(BF)
    cuts = pieces_of(D)
    gathers = []
    for p, (at, end) in enumerate(cuts):
        cols = pl.ds(at, end - at)
        for k in range(1, n_tp):
            peer = lax.rem(my + k, n_tp)
            mine = normed.at[my, :, cols]
            c = remote(mine, mine, ag_send.at[p, k], ag_recv.at[p, k], "tp", peer)
            c.start()
            gathers.append(c)
    sends = []
    for p, (at, end) in enumerate(cuts):
        cols = pl.ds(at, end - at)
        for k in range(1, n_tp):
            gathers[p * (n_tp - 1) + k - 1].wait_recv()
        tokens = normed[:, :, at:end].reshape(n_tp * chunk, end - at)
        picked = jnp.dot(route[...], tokens, preferred_element_type=F32)
        for e in range(EXPERTS):
            out_buf[e, :, at:end] = picked[e * CAP : (e + 1) * CAP].astype(BF)
        for k in range(1, n_req):
            peer = lax.rem(me + k, n_req)
            c = remote(
                out_buf.at[peer // split, :, cols],
                rows.at[me, :, cols],
                a2a_send.at[p, k],
                a2a_recv.at[p, k],
                "req",
                peer,
            )
            c.start()
            sends.append(c)
        rows[me, :, at:end] = out_buf[me // split, :, at:end]
    for c in sends:
        c.wait_recv()
    for c in copies + gathers + sends:
        c.wait_send()


def dispatch(term, act, gain, route, n_tp, n_req):
    T, D = term.shape
    chunk = T // n_tp
    vmem = pl.BlockSpec(memory_space=pltpu.VMEM)
    dma = pltpu.SemaphoreType.DMA
    rows, normed, res = pl.pallas_call(
        functools.partial(dispatch_kernel, n_tp, n_req),
        out_shape=(
            jax.ShapeDtypeStruct((n_req, CAP, D), BF),
            jax.ShapeDtypeStruct((n_tp, chunk, D), BF),
            jax.ShapeDtypeStruct((chunk, D), F32),
        ),
        in_specs=[vmem] * 4,
        out_specs=(vmem, vmem, vmem),
        scratch_shapes=[
            pltpu.VMEM((n_tp - 1, chunk, D), BF),
            pltpu.VMEM((EXPERTS, CAP, D), BF),
            dma((n_tp,)),
            dma((n_tp,)),
            dma((PIECES, n_tp)),
            dma((PIECES, n_tp)),
            dma((PIECES, n_req)),
            dma((PIECES, n_req)),
        ],
        compiler_params=pltpu.CompilerParams(
            collective_id=1, has_side_effects=True, vmem_limit_bytes=VMEM_BYTES
        ),
    )(term.reshape(n_tp, chunk, D), act, gain, route)
    return rows.reshape(n_req * CAP, D), normed.reshape(T, D), res


def collect_kernel(
    n_tp, n_req, part, high, low, res, out, back, moe, rs_buf,
    a2a_send, a2a_recv, rs_send, rs_recv, ag_send, ag_recv,
):
    my, me = lax.axis_index("tp"), lax.axis_index("req")
    chunk, D = res.shape
    cuts = pieces_of(D)
    greet(True, True, n_tp, n_req)
    arrivals, sums, gathers = [], [[] for _ in cuts], []
    for p, (at, end) in enumerate(cuts):
        cols = pl.ds(at, end - at)
        for k in range(1, n_req):
            peer = lax.rem(me + k, n_req)
            c = remote(
                part.at[peer, :, cols],
                back.at[me, :, cols],
                a2a_send.at[p, k],
                a2a_recv.at[p, k],
                "req",
                peer,
            )
            c.start()
            arrivals.append(c)
    back[me] = part[me]

    def combine(p):
        at, end = cuts[p]
        cols = pl.ds(at, end - at)
        for k in range(1, n_req):
            arrivals[p * (n_req - 1) + k - 1].wait_recv()
        x = back[:, :, at:end].astype(F32).reshape(n_req * CAP, end - at).astype(BF)
        y = jnp.dot(high[...], x, preferred_element_type=F32)
        y = y + jnp.dot(low[...], x, preferred_element_type=F32)
        moe[:, :, at:end] = y.astype(BF).reshape(n_tp, chunk, end - at)
        for k in range(1, n_tp):
            peer = lax.rem(my + k, n_tp)
            c = remote(
                moe.at[peer, :, cols],
                rs_buf.at[k - 1, :, cols],
                rs_send.at[p, k],
                rs_recv.at[p, k],
                "tp",
                peer,
            )
            c.start()
            sums[p].append(c)

    def finish(p):
        at, end = cuts[p]
        cols = pl.ds(at, end - at)
        for c in sums[p]:
            c.wait_recv()
        y = moe[my, :, at:end].astype(F32)
        for k in range(1, n_tp):
            y = y + rs_buf[k - 1, :, at:end].astype(F32)
        out[my, :, at:end] = (res[:, at:end] + y).astype(BF)
        for k in range(1, n_tp):
            peer = lax.rem(my + k, n_tp)
            mine = out.at[my, :, cols]
            c = remote(mine, mine, ag_send.at[p, k], ag_recv.at[p, k], "tp", peer)
            c.start()
            gathers.append(c)

    for p in range(len(cuts)):
        combine(p)
        if p > 0:
            finish(p - 1)
    finish(len(cuts) - 1)
    for c in gathers:
        c.wait_recv()
    for c in arrivals + sum(sums, []) + gathers:
        c.wait_send()


def collect(part, high, low, res, n_tp, n_req):
    chunk, D = res.shape
    vmem = pl.BlockSpec(memory_space=pltpu.VMEM)
    dma = pltpu.SemaphoreType.DMA
    out = pl.pallas_call(
        functools.partial(collect_kernel, n_tp, n_req),
        out_shape=jax.ShapeDtypeStruct((n_tp, chunk, D), BF),
        in_specs=[vmem] * 4,
        out_specs=vmem,
        scratch_shapes=[
            pltpu.VMEM((n_req, CAP, D), BF),
            pltpu.VMEM((n_tp, chunk, D), BF),
            pltpu.VMEM((n_tp - 1, chunk, D), BF),
            dma((PIECES, n_req)),
            dma((PIECES, n_req)),
            dma((PIECES, n_tp)),
            dma((PIECES, n_tp)),
            dma((PIECES, n_tp)),
            dma((PIECES, n_tp)),
        ],
        compiler_params=pltpu.CompilerParams(
            collective_id=2, has_side_effects=True, vmem_limit_bytes=VMEM_BYTES
        ),
    )(part.reshape(n_req, CAP, D), high, low, res)
    return out.reshape(n_tp * chunk, D)


def per_device(
    activations,
    lengths,
    adapter_of,
    slot_of,
    page_table,
    experts_of,
    attn_gain,
    moe_gain,
    w_qkv,
    output_weight,
    router,
    w_gate_up,
    w_down,
    expert_up_factors,
    pool_a,
    slot_query_key_value_up,
    pool_aout,
    pool_bout,
):
    T, D = activations.shape
    n_req = lax.axis_size("req")
    n_tp = lax.axis_size("tp")
    R = ADAPTER_RANK
    width = w_qkv.shape[2]
    heads = width // HEAD_SIZE
    own = pool_a.shape[0]
    n_slots = own * n_req
    n_adapters = slot_of.shape[0]
    share = D // n_tp
    pad = -share % 128
    pad_w = -width % 128

    my_tp = lax.axis_index("tp")
    down_t = pool_a.transpose(0, 2, 1)
    down_part = lax.dynamic_slice_in_dim(down_t[:, : 3 * R], my_tp * share, share, 2)
    up_t = slot_query_key_value_up.transpose(0, 2, 1, 3).reshape(own, 3 * R, width)
    aout_t = pool_aout.transpose(0, 2, 1)
    pool_down = lax.all_gather(
        jnp.pad(down_part, ((0, 0), (0, 0), (0, pad))), "req", axis=0, tiled=True
    )[:, :, :share]
    pool_up = lax.all_gather(
        jnp.pad(jnp.concatenate([up_t, aout_t], axis=1), ((0, 0), (0, 0), (0, pad_w))),
        "req",
        axis=0,
        tiled=True,
    )[:, :, :width]
    pool_late = lax.all_gather(
        jnp.concatenate([down_t[:, 3 * R :], pool_bout], axis=1), "req", axis=0, tiled=True
    )
    pool_exp, pool_bup = pool_late[:, :R], pool_late[:, R:]

    row = lengths[0]
    n_in = row.shape[0]
    ends = jnp.sum(jnp.where(iota((n_in, n_in), 0) <= iota((n_in, n_in), 1), row[:, None], 0), axis=0)
    starts = ends - row
    pages = (row + PAGE - 1) // PAGE
    first_page = jnp.sum(
        jnp.where(iota((n_in, n_in), 0) < iota((n_in, n_in), 1), pages[:, None], 0), axis=0
    )
    slots_in = jnp.sum(
        jnp.where(
            adapter_of[0][:, None] == iota((n_in, n_adapters), 1), slot_of[None, :], 0
        ),
        axis=1,
    )
    place = iota((T, n_in), 0)
    here = (place >= starts[None, :]) & (place < ends[None, :])

    def of_request(values):
        return jnp.sum(jnp.where(here, values[None, :], 0), axis=1, keepdims=True)

    start = of_request(starts)
    token_slot = of_request(slots_in)
    adapter = of_request(adapter_of[0])
    position = iota((T, 1), 0) - start
    page_at = of_request(first_page) + position // PAGE
    n_pages = page_table.shape[1]
    local_page = jnp.sum(
        jnp.where(page_at == iota((T, n_pages), 1), page_table, 0), axis=1, keepdims=True
    )
    cache_row = local_page * PAGE + position % PAGE

    def slot_mask(each):
        return token_slot == iota((T, n_slots * each), 1) // each

    mask_r = slot_mask(R)

    act = activations.astype(F32)
    mean_sq = jnp.mean(act * act, axis=-1, keepdims=True)
    normed = (act * lax.rsqrt(mean_sq + epsilon) * attn_gain).astype(BF)
    normed = lax.optimization_barrier(normed)
    plain = [dot_nt(w_qkv[:, p].T, normed) for p in range(3)]
    normed_part = lax.dynamic_slice_in_dim(normed, my_tp * share, share, 1)
    coeff_mask = slot_mask(1)
    down_all = dot_nt(
        pool_down.transpose(1, 0, 2).reshape(3 * R * n_slots, share), normed_part
    ).reshape(3 * R, n_slots, T)
    slot_row = coeff_mask.T
    coeff_part = jnp.sum(jnp.where(slot_row[None], down_all, 0.0), axis=1)
    coeff = small_sum(coeff_part, n_tp).astype(BF)

    projected = []
    for p in range(3):
        spread = jnp.where(
            slot_row[:, None, :],
            coeff[p * R : (p + 1) * R][None] * jnp.array(adapter_scale, BF),
            jnp.zeros((), BF),
        ).reshape(n_slots * R, T)
        up = pool_up[:, p * R : (p + 1) * R].reshape(n_slots * R, width)
        projected.append(plain[p] + dot_tn(up, spread))

    tables = jnp.asarray(rope_tables(T))
    hot = (position == iota((T, T), 1)).astype(BF)
    turned = lax.dot_general(
        tables,
        jnp.concatenate([hot, hot, hot], axis=1),
        (((0,), (1,)), ((), ())),
        preferred_element_type=F32,
    )
    half = HEAD_SIZE // 2
    cosine, sine = turned[None, :half], turned[None, half:]

    def rotate(x):
        x = x.reshape(heads, HEAD_SIZE, T)
        front, back = x[:, :half], x[:, half:]
        return jnp.concatenate(
            [front * cosine - back * sine, back * cosine + front * sine], axis=1
        ).astype(BF)

    queries = rotate(projected[0])
    keys = rotate(projected[1])
    values = projected[2].astype(BF).reshape(heads, HEAD_SIZE, T)

    place_hot = (cache_row == iota((T, n_pages * PAGE), 1)).astype(BF)
    cache = [
        lax.dot_general(
            place_hot, x.reshape(width, T), (((0,), (1,)), ((), ())), preferred_element_type=F32
        )
        .astype(BF)
        .reshape(n_pages, PAGE, width)
        for x in (keys, values)
    ]
    page_cache = jnp.stack(cache, axis=2)

    scores = jnp.einsum("hdq,hdk->hqk", queries, keys, preferred_element_type=F32) * (
        1.0 / math.sqrt(HEAD_SIZE)
    )
    seen = iota((T, T), 1)
    allowed = (seen <= iota((T, T), 0)) & (seen >= start)
    scores = jnp.where(allowed[None], scores, -1e30)
    weights = jnp.exp(scores - jnp.max(scores, axis=-1, keepdims=True))
    weights = (weights / jnp.sum(weights, axis=-1, keepdims=True)).astype(BF)
    attended = (
        jnp.einsum("hqk,hdk->qhd", weights, values, preferred_element_type=F32)
        .astype(BF)
        .reshape(T, width)
    )

    aout_all = dot_nt(attended, pool_up[:, 3 * R :].reshape(n_slots * R, width))
    spread_hi, spread_lo = split_two(jnp.where(mask_r, adapter_scale * aout_all, 0.0))
    bup = pool_bup.reshape(n_slots * R, D)
    term = dot(attended, output_weight) + dot(
        jnp.concatenate([spread_hi, spread_lo], axis=1), jnp.concatenate([bup, bup], axis=0)
    )

    split = n_req // EXPERTS
    experts = [experts_of[:, k : k + 1] for k in range(2)]
    hots = [e == iota((T, EXPERTS), 1) for e in experts]
    chosen_any = (hots[0] | hots[1]).astype(BF)
    before = (iota((T, T), 1) < iota((T, T), 0)).astype(BF)
    prior = dot(before, chosen_any).astype(jnp.int32)
    picks = []
    for k in range(2):
        order = jnp.sum(jnp.where(hots[k], prior, 0), axis=1, keepdims=True)
        picks.append(experts[k] * CAP + order == iota((T, EXPERTS * CAP), 1))
    route = (picks[0] | picks[1]).astype(BF)

    def send(x):
        rows = dot_tn(route, x).astype(BF).reshape(EXPERTS, 1, CAP, x.shape[1])
        rows = jnp.broadcast_to(rows, (EXPERTS, split, CAP, x.shape[1]))
        got = lax.all_to_all(
            rows.reshape(n_req, CAP, x.shape[1]), "req", split_axis=0, concat_axis=0, tiled=True
        )
        return got.reshape(n_req * CAP, x.shape[1])

    units = w_gate_up.shape[3]
    chunk = T // n_tp
    rows, normed_moe, res = dispatch(
        term.astype(BF),
        lax.dynamic_slice_in_dim(activations, my_tp * chunk, chunk, 0),
        moe_gain[None],
        route.T,
        n_tp,
        n_req,
    )
    exp_all = dot_nt(normed_moe, pool_exp.reshape(n_slots * R, D))
    logits = dot(normed_moe, router)
    coeff_exp = jnp.where(mask_r, exp_all, 0.0).astype(BF)
    fold = (iota((n_slots * R, R), 0) % R == iota((n_slots * R, R), 1)).astype(BF)
    coeff_exp = dot(coeff_exp, fold).astype(BF)
    meta = jnp.concatenate([coeff_exp, adapter.astype(BF)], axis=1)
    got = send(meta)
    got_coeff = got[:, :R]
    got_ids = got[:, R : R + 1].astype(jnp.int32)
    unfold = (iota((R, n_adapters * R), 1) % R == iota((R, n_adapters * R), 0)).astype(BF)
    broad = dot(got_coeff * jnp.array(adapter_scale, BF), unfold)
    broad = jnp.where(
        got_ids == iota((n_req * CAP, n_adapters * R), 1) // R, broad, 0.0
    ).astype(BF)
    before_act = dot(rows, w_gate_up[0].reshape(D, 2 * units)) + dot(
        broad, expert_up_factors[0].reshape(n_adapters * R, 2 * units)
    )
    hidden = (jax.nn.silu(before_act[:, :units]) * before_act[:, units:]).astype(BF)

    chosen = [
        jnp.sum(jnp.where(hots[k], logits, 0.0), axis=1, keepdims=True) for k in range(2)
    ]
    gates = [1.0 / (1.0 + jnp.exp(chosen[1 - k] - chosen[k])) for k in range(2)]
    combine = jnp.where(picks[0], gates[0], 0.0) + jnp.where(picks[1], gates[1], 0.0)
    combine = jnp.broadcast_to(
        combine.reshape(T, EXPERTS, 1, CAP), (T, EXPERTS, split, CAP)
    ).reshape(T, n_req * CAP)
    combine_hi, combine_lo = split_two(combine)

    part = dot(hidden, w_down[0]).astype(BF)
    layer_out = collect(part, combine_hi, combine_lo, res, n_tp, n_req)
    return (layer_out, page_cache)


def solution(mesh):
    return jax.shard_map(
        per_device,
        mesh=mesh,
        in_specs=(
            P("req", None),
            P("req", None),
            P("req", None),
            P(),
            P("req", None),
            P("req", None),
            P(),
            P(),
            P(None, None, "tp"),
            P("tp", None),
            P(),
            P("req", None, None, "tp"),
            P("req", "tp", None),
            P("req", None, None, "tp"),
            P("req", None, None),
            P("req", None, None, "tp"),
            P("req", "tp", None),
            P("req", None, None),
        ),
        out_specs=(P("req", None), P("req", None, None, "tp")),
        check_vma=False,
    )
```

```python
import functools
import math

import jax
import jax.numpy as jnp
import numpy as np
from jax import lax
from jax.experimental import pallas as pl
from jax.experimental.pallas import tpu as pltpu
from jax.sharding import PartitionSpec as P

HEAD_SIZE = 64
EXPERTS = 8
ADAPTER_RANK = 16
PAGE = 128
CAP = 72
PIECES = 3
MESH = pl.DeviceIdType.MESH
VMEM_BYTES = 20 * 2**20

epsilon = 1e-05
adapter_scale = 2.0
rope_base = 10000.0

BF = jnp.bfloat16
F32 = jnp.float32


def iota(shape, dim):
    return lax.broadcasted_iota(jnp.int32, shape, dim)


def dot(a, b):
    return jnp.dot(a, b, preferred_element_type=F32)


def dot_nt(a, b):
    return lax.dot_general(a, b, (((1,), (1,)), ((), ())), preferred_element_type=F32)


def dot_tn(a, b):
    return lax.dot_general(a, b, (((0,), (0,)), ((), ())), preferred_element_type=F32)


def split_two(x):
    high = lax.reduce_precision(x, 8, 7)
    return high.astype(BF), (x - high).astype(BF)


def rope_tables(count):
    half = HEAD_SIZE // 2
    frequency = np.float32(rope_base) ** (-np.arange(half, dtype=np.float32) * np.float32(2.0) / HEAD_SIZE)
    angles = np.arange(count, dtype=np.float32)[:, None] * frequency[None, :].astype(np.float32)
    table = np.concatenate([np.cos(angles), np.sin(angles)], axis=1).astype(np.float32)
    parts = []
    for _ in range(3):
        part = table.astype(BF)
        parts.append(part)
        table = table - part.astype(np.float32)
    return np.concatenate(parts, axis=0)


def pieces_of(width):
    units = width // 128
    sizes = [(units * (i + 1)) // PIECES - (units * i) // PIECES for i in range(PIECES)]
    sizes[-1] += 0
    cuts, at = [], 0
    for i, size in enumerate(sizes):
        end = width if i == PIECES - 1 else at + size * 128
        cuts.append((at, end))
        at = end
    return cuts


def greet(tp_too, req_too, n_tp, n_req):
    barrier = pltpu.get_barrier_semaphore()
    count = 0
    for axis, n, wanted in (("tp", n_tp, tp_too), ("req", n_req, req_too)):
        if wanted:
            me = lax.axis_index(axis)
            for k in range(1, n):
                pl.semaphore_signal(
                    barrier, inc=1, device_id={axis: lax.rem(me + k, n)}, device_id_type=MESH
                )
            count += n - 1
    pl.semaphore_wait(barrier, count)


def remote(src, dst, send_sem, recv_sem, axis, peer):
    return pltpu.make_async_remote_copy(
        src_ref=src,
        dst_ref=dst,
        send_sem=send_sem,
        recv_sem=recv_sem,
        device_id={axis: peer},
        device_id_type=MESH,
    )


def small_sum_kernel(n_tp, x_ref, o_ref, buf, send, recv):
    me = lax.axis_index("tp")
    greet(True, False, n_tp, 1)
    copies = []
    for k in range(1, n_tp):
        c = remote(x_ref, buf.at[k - 1], send.at[k], recv.at[k], "tp", lax.rem(me + k, n_tp))
        c.start()
        copies.append(c)
    total = x_ref[...]
    for c in copies:
        c.wait_recv()
    for k in range(1, n_tp):
        total = total + buf[k - 1]
    o_ref[...] = total
    for c in copies:
        c.wait_send()


def small_sum(x, n_tp):
    return pl.pallas_call(
        functools.partial(small_sum_kernel, n_tp),
        out_shape=jax.ShapeDtypeStruct(x.shape, x.dtype),
        in_specs=[pl.BlockSpec(memory_space=pltpu.VMEM)],
        out_specs=pl.BlockSpec(memory_space=pltpu.VMEM),
        scratch_shapes=[
            pltpu.VMEM((n_tp - 1,) + x.shape, x.dtype),
            pltpu.SemaphoreType.DMA((n_tp,)),
            pltpu.SemaphoreType.DMA((n_tp,)),
        ],
        compiler_params=pltpu.CompilerParams(
            collective_id=0, has_side_effects=True, vmem_limit_bytes=VMEM_BYTES
        ),
    )(x)


def dispatch_kernel(
    n_tp, n_req, term, act, gain, route, rows, normed, res, rs_buf, out_buf,
    rs_send, rs_recv, ag_send, ag_recv, a2a_send, a2a_recv,
):
    my, me = lax.axis_index("tp"), lax.axis_index("req")
    chunk, D = act.shape
    split = n_req // EXPERTS
    greet(True, True, n_tp, n_req)
    copies = []
    for k in range(1, n_tp):
        peer = lax.rem(my + k, n_tp)
        c = remote(term.at[peer], rs_buf.at[k - 1], rs_send.at[k], rs_recv.at[k], "tp", peer)
        c.start()
        copies.append(c)
    total = act[...].astype(F32) + term[my].astype(F32)
    for k in range(1, n_tp):
        copies[k - 1].wait_recv()
        total = total + rs_buf[k - 1].astype(F32)
    res[...] = total
    mean_sq = jnp.mean(total * total, axis=-1, keepdims=True)
    normed[my] = (total * lax.rsqrt(mean_sq + epsilon) * gain[...]).astype(BF)
    cuts = pieces_of(D)
    gathers = []
    for p, (at, end) in enumerate(cuts):
        cols = pl.ds(at, end - at)
        for k in range(1, n_tp):
            peer = lax.rem(my + k, n_tp)
            mine = normed.at[my, :, cols]
            c = remote(mine, mine, ag_send.at[p, k], ag_recv.at[p, k], "tp", peer)
            c.start()
            gathers.append(c)
    sends = []
    for p, (at, end) in enumerate(cuts):
        cols = pl.ds(at, end - at)
        for k in range(1, n_tp):
            gathers[p * (n_tp - 1) + k - 1].wait_recv()
        tokens = normed[:, :, at:end].reshape(n_tp * chunk, end - at)
        picked = jnp.dot(route[...], tokens, preferred_element_type=F32)
        for e in range(EXPERTS):
            out_buf[e, :, at:end] = picked[e * CAP : (e + 1) * CAP].astype(BF)
        for k in range(1, n_req):
            peer = lax.rem(me + k, n_req)
            c = remote(
                out_buf.at[peer // split, :, cols],
                rows.at[me, :, cols],
                a2a_send.at[p, k],
                a2a_recv.at[p, k],
                "req",
                peer,
            )
            c.start()
            sends.append(c)
        rows[me, :, at:end] = out_buf[me // split, :, at:end]
    for c in sends:
        c.wait_recv()
    for c in copies + gathers + sends:
        c.wait_send()


def dispatch(term, act, gain, route, n_tp, n_req):
    T, D = term.shape
    chunk = T // n_tp
    vmem = pl.BlockSpec(memory_space=pltpu.VMEM)
    dma = pltpu.SemaphoreType.DMA
    rows, normed, res = pl.pallas_call(
        functools.partial(dispatch_kernel, n_tp, n_req),
        out_shape=(
            jax.ShapeDtypeStruct((n_req, CAP, D), BF),
            jax.ShapeDtypeStruct((n_tp, chunk, D), BF),
            jax.ShapeDtypeStruct((chunk, D), F32),
        ),
        in_specs=[vmem] * 4,
        out_specs=(vmem, vmem, vmem),
        scratch_shapes=[
            pltpu.VMEM((n_tp - 1, chunk, D), BF),
            pltpu.VMEM((EXPERTS, CAP, D), BF),
            dma((n_tp,)),
            dma((n_tp,)),
            dma((PIECES, n_tp)),
            dma((PIECES, n_tp)),
            dma((PIECES, n_req)),
            dma((PIECES, n_req)),
        ],
        compiler_params=pltpu.CompilerParams(
            collective_id=1, has_side_effects=True, vmem_limit_bytes=VMEM_BYTES
        ),
    )(term.reshape(n_tp, chunk, D), act, gain, route)
    return rows.reshape(n_req * CAP, D), normed.reshape(T, D), res


def collect_kernel(
    n_tp, n_req, part, high, low, res, out, back, moe, rs_buf,
    a2a_send, a2a_recv, rs_send, rs_recv, ag_send, ag_recv,
):
    my, me = lax.axis_index("tp"), lax.axis_index("req")
    chunk, D = res.shape
    cuts = pieces_of(D)
    greet(True, True, n_tp, n_req)
    arrivals, sums, gathers = [], [[] for _ in cuts], []
    for p, (at, end) in enumerate(cuts):
        cols = pl.ds(at, end - at)
        for k in range(1, n_req):
            peer = lax.rem(me + k, n_req)
            c = remote(
                part.at[peer, :, cols],
                back.at[me, :, cols],
                a2a_send.at[p, k],
                a2a_recv.at[p, k],
                "req",
                peer,
            )
            c.start()
            arrivals.append(c)
    back[me] = part[me]

    def combine(p):
        at, end = cuts[p]
        cols = pl.ds(at, end - at)
        for k in range(1, n_req):
            arrivals[p * (n_req - 1) + k - 1].wait_recv()
        x = back[:, :, at:end].astype(F32).reshape(n_req * CAP, end - at).astype(BF)
        y = jnp.dot(high[...], x, preferred_element_type=F32)
        y = y + jnp.dot(low[...], x, preferred_element_type=F32)
        moe[:, :, at:end] = y.astype(BF).reshape(n_tp, chunk, end - at)
        for k in range(1, n_tp):
            peer = lax.rem(my + k, n_tp)
            c = remote(
                moe.at[peer, :, cols],
                rs_buf.at[k - 1, :, cols],
                rs_send.at[p, k],
                rs_recv.at[p, k],
                "tp",
                peer,
            )
            c.start()
            sums[p].append(c)

    def finish(p):
        at, end = cuts[p]
        cols = pl.ds(at, end - at)
        for c in sums[p]:
            c.wait_recv()
        y = moe[my, :, at:end].astype(F32)
        for k in range(1, n_tp):
            y = y + rs_buf[k - 1, :, at:end].astype(F32)
        out[my, :, at:end] = (res[:, at:end] + y).astype(BF)
        for k in range(1, n_tp):
            peer = lax.rem(my + k, n_tp)
            mine = out.at[my, :, cols]
            c = remote(mine, mine, ag_send.at[p, k], ag_recv.at[p, k], "tp", peer)
            c.start()
            gathers.append(c)

    for p in range(len(cuts)):
        combine(p)
        if p > 0:
            finish(p - 1)
    finish(len(cuts) - 1)
    for c in gathers:
        c.wait_recv()
    for c in arrivals + sum(sums, []) + gathers:
        c.wait_send()


def collect(part, high, low, res, n_tp, n_req):
    chunk, D = res.shape
    vmem = pl.BlockSpec(memory_space=pltpu.VMEM)
    dma = pltpu.SemaphoreType.DMA
    out = pl.pallas_call(
        functools.partial(collect_kernel, n_tp, n_req),
        out_shape=jax.ShapeDtypeStruct((n_tp, chunk, D), BF),
        in_specs=[vmem] * 4,
        out_specs=vmem,
        scratch_shapes=[
            pltpu.VMEM((n_req, CAP, D), BF),
            pltpu.VMEM((n_tp, chunk, D), BF),
            pltpu.VMEM((n_tp - 1, chunk, D), BF),
            dma((PIECES, n_req)),
            dma((PIECES, n_req)),
            dma((PIECES, n_tp)),
            dma((PIECES, n_tp)),
            dma((PIECES, n_tp)),
            dma((PIECES, n_tp)),
        ],
        compiler_params=pltpu.CompilerParams(
            collective_id=2, has_side_effects=True, vmem_limit_bytes=VMEM_BYTES
        ),
    )(part.reshape(n_req, CAP, D), high, low, res)
    return out.reshape(n_tp * chunk, D)


def per_device(
    activations,
    lengths,
    adapter_of,
    slot_of,
    page_table,
    experts_of,
    attn_gain,
    moe_gain,
    w_qkv,
    output_weight,
    router,
    w_gate_up,
    w_down,
    expert_up_factors,
    pool_a,
    slot_query_key_value_up,
    pool_aout,
    pool_bout,
):
    T, D = activations.shape
    n_req = lax.axis_size("req")
    n_tp = lax.axis_size("tp")
    R = ADAPTER_RANK
    width = w_qkv.shape[2]
    heads = width // HEAD_SIZE
    own = pool_a.shape[0]
    n_slots = own * n_req
    n_adapters = slot_of.shape[0]
    share = D // n_tp
    pad = -share % 128
    pad_w = -width % 128

    my_tp = lax.axis_index("tp")
    down_t = pool_a.transpose(0, 2, 1)
    down_part = lax.dynamic_slice_in_dim(down_t[:, : 3 * R], my_tp * share, share, 2)
    up_t = slot_query_key_value_up.transpose(0, 2, 1, 3).reshape(own, 3 * R, width)
    aout_t = pool_aout.transpose(0, 2, 1)
    pool_down = lax.all_gather(
        jnp.pad(down_part, ((0, 0), (0, 0), (0, pad))), "req", axis=0, tiled=True
    )[:, :, :share]
    pool_up = lax.all_gather(
        jnp.pad(jnp.concatenate([up_t, aout_t], axis=1), ((0, 0), (0, 0), (0, pad_w))),
        "req",
        axis=0,
        tiled=True,
    )[:, :, :width]
    pool_late = lax.all_gather(
        jnp.concatenate([down_t[:, 3 * R :], pool_bout], axis=1), "req", axis=0, tiled=True
    )
    pool_exp, pool_bup = pool_late[:, :R], pool_late[:, R:]

    row = lengths[0]
    n_in = row.shape[0]
    ends = jnp.sum(jnp.where(iota((n_in, n_in), 0) <= iota((n_in, n_in), 1), row[:, None], 0), axis=0)
    starts = ends - row
    pages = (row + PAGE - 1) // PAGE
    first_page = jnp.sum(
        jnp.where(iota((n_in, n_in), 0) < iota((n_in, n_in), 1), pages[:, None], 0), axis=0
    )
    slots_in = jnp.sum(
        jnp.where(
            adapter_of[0][:, None] == iota((n_in, n_adapters), 1), slot_of[None, :], 0
        ),
        axis=1,
    )
    place = iota((T, n_in), 0)
    here = (place >= starts[None, :]) & (place < ends[None, :])

    def of_request(values):
        return jnp.sum(jnp.where(here, values[None, :], 0), axis=1, keepdims=True)

    start = of_request(starts)
    token_slot = of_request(slots_in)
    adapter = of_request(adapter_of[0])
    position = iota((T, 1), 0) - start
    page_at = of_request(first_page) + position // PAGE
    n_pages = page_table.shape[1]
    local_page = jnp.sum(
        jnp.where(page_at == iota((T, n_pages), 1), page_table, 0), axis=1, keepdims=True
    )
    cache_row = local_page * PAGE + position % PAGE

    def slot_mask(each):
        return token_slot == iota((T, n_slots * each), 1) // each

    mask_r = slot_mask(R)

    act = activations.astype(F32)
    mean_sq = jnp.mean(act * act, axis=-1, keepdims=True)
    normed = (act * lax.rsqrt(mean_sq + epsilon) * attn_gain).astype(BF)
    normed = lax.optimization_barrier(normed)
    plain = [dot_nt(w_qkv[:, p].T, normed) for p in range(3)]
    normed_part = lax.dynamic_slice_in_dim(normed, my_tp * share, share, 1)
    coeff_mask = slot_mask(1)
    down_all = dot_nt(
        pool_down.transpose(1, 0, 2).reshape(3 * R * n_slots, share), normed_part
    ).reshape(3 * R, n_slots, T)
    slot_row = coeff_mask.T
    coeff_part = jnp.sum(jnp.where(slot_row[None], down_all, 0.0), axis=1)
    coeff = small_sum(coeff_part, n_tp).astype(BF)

    projected = []
    for p in range(3):
        spread = jnp.where(
            slot_row[:, None, :],
            coeff[p * R : (p + 1) * R][None] * jnp.array(adapter_scale, BF),
            jnp.zeros((), BF),
        ).reshape(n_slots * R, T)
        up = pool_up[:, p * R : (p + 1) * R].reshape(n_slots * R, width)
        projected.append(plain[p] + dot_tn(up, spread))

    tables = jnp.asarray(rope_tables(T))
    hot = (position == iota((T, T), 1)).astype(BF)
    turned = lax.dot_general(
        tables,
        jnp.concatenate([hot, hot, hot], axis=1),
        (((0,), (1,)), ((), ())),
        preferred_element_type=F32,
    )
    half = HEAD_SIZE // 2
    cosine, sine = turned[None, :half], turned[None, half:]

    def rotate(x):
        x = x.reshape(heads, HEAD_SIZE, T)
        front, back = x[:, :half], x[:, half:]
        return jnp.concatenate(
            [front * cosine - back * sine, back * cosine + front * sine], axis=1
        ).astype(BF)

    queries = rotate(projected[0])
    keys = rotate(projected[1])
    values = projected[2].astype(BF).reshape(heads, HEAD_SIZE, T)

    place_hot = (cache_row == iota((T, n_pages * PAGE), 1)).astype(BF)
    key_value = jnp.concatenate([keys.reshape(width, T), values.reshape(width, T)], axis=0)
    page_cache = (
        lax.dot_general(
            place_hot.T.reshape(n_pages, PAGE, T),
            key_value,
            (((2,), (1,)), ((), ())),
            preferred_element_type=F32,
        )
        .astype(BF)
        .reshape(n_pages, PAGE, 2, width)
    )

    scores = jnp.einsum("hdq,hdk->hqk", queries, keys, preferred_element_type=F32) * (
        1.0 / math.sqrt(HEAD_SIZE)
    )
    seen = iota((T, T), 1)
    allowed = (seen <= iota((T, T), 0)) & (seen >= start)
    scores = jnp.where(allowed[None], scores, -1e30)
    weights = jnp.exp(scores - jnp.max(scores, axis=-1, keepdims=True))
    weights = (weights / jnp.sum(weights, axis=-1, keepdims=True)).astype(BF)
    attended = (
        jnp.einsum("hqk,hdk->qhd", weights, values, preferred_element_type=F32)
        .astype(BF)
        .reshape(T, width)
    )

    aout_all = dot_nt(attended, pool_up[:, 3 * R :].reshape(n_slots * R, width))
    spread_hi, spread_lo = split_two(jnp.where(mask_r, adapter_scale * aout_all, 0.0))
    bup = pool_bup.reshape(n_slots * R, D)
    term = dot(attended, output_weight) + dot(
        jnp.concatenate([spread_hi, spread_lo], axis=1), jnp.concatenate([bup, bup], axis=0)
    )

    split = n_req // EXPERTS
    experts = [experts_of[:, k : k + 1] for k in range(2)]
    hots = [e == iota((T, EXPERTS), 1) for e in experts]
    chosen_any = (hots[0] | hots[1]).astype(BF)
    before = (iota((T, T), 1) < iota((T, T), 0)).astype(BF)
    prior = dot(before, chosen_any).astype(jnp.int32)
    picks = []
    for k in range(2):
        order = jnp.sum(jnp.where(hots[k], prior, 0), axis=1, keepdims=True)
        picks.append(experts[k] * CAP + order == iota((T, EXPERTS * CAP), 1))
    route = (picks[0] | picks[1]).astype(BF)

    def send(x):
        rows = dot_tn(route, x).astype(BF).reshape(EXPERTS, 1, CAP, x.shape[1])
        rows = jnp.broadcast_to(rows, (EXPERTS, split, CAP, x.shape[1]))
        got = lax.all_to_all(
            rows.reshape(n_req, CAP, x.shape[1]), "req", split_axis=0, concat_axis=0, tiled=True
        )
        return got.reshape(n_req * CAP, x.shape[1])

    units = w_gate_up.shape[3]
    chunk = T // n_tp
    rows, normed_moe, res = dispatch(
        term.astype(BF),
        lax.dynamic_slice_in_dim(activations, my_tp * chunk, chunk, 0),
        moe_gain[None],
        route.T,
        n_tp,
        n_req,
    )
    exp_all = dot_nt(normed_moe, pool_exp.reshape(n_slots * R, D))
    logits = dot(normed_moe, router)
    coeff_exp = jnp.where(mask_r, exp_all, 0.0).astype(BF)
    fold = (iota((n_slots * R, R), 0) % R == iota((n_slots * R, R), 1)).astype(BF)
    coeff_exp = dot(coeff_exp, fold).astype(BF)
    meta = jnp.concatenate([coeff_exp, adapter.astype(BF)], axis=1)
    got = send(meta)
    got_coeff = got[:, :R]
    got_ids = got[:, R : R + 1].astype(jnp.int32)
    unfold = (iota((R, n_adapters * R), 1) % R == iota((R, n_adapters * R), 0)).astype(BF)
    broad = dot(got_coeff, unfold)
    broad = jnp.where(
        got_ids == iota((n_req * CAP, n_adapters * R), 1) // R, broad, 0.0
    ).astype(BF)
    before_act = dot(rows, w_gate_up[0].reshape(D, 2 * units)) + adapter_scale * dot(
        broad, expert_up_factors[0].reshape(n_adapters * R, 2 * units)
    )
    hidden = (jax.nn.silu(before_act[:, :units]) * before_act[:, units:]).astype(BF)

    chosen = [
        jnp.sum(jnp.where(hots[k], logits, 0.0), axis=1, keepdims=True) for k in range(2)
    ]
    gates = [1.0 / (1.0 + jnp.exp(chosen[1 - k] - chosen[k])) for k in range(2)]
    combine = jnp.where(picks[0], gates[0], 0.0) + jnp.where(picks[1], gates[1], 0.0)
    combine = jnp.broadcast_to(
        combine.reshape(T, EXPERTS, 1, CAP), (T, EXPERTS, split, CAP)
    ).reshape(T, n_req * CAP)
    combine_hi, combine_lo = split_two(combine)

    part = dot(hidden, w_down[0]).astype(BF)
    layer_out = collect(part, combine_hi, combine_lo, res, n_tp, n_req)
    return (layer_out, page_cache)


def solution(mesh):
    return jax.shard_map(
        per_device,
        mesh=mesh,
        in_specs=(
            P("req", None),
            P("req", None),
            P("req", None),
            P(),
            P("req", None),
            P("req", None),
            P(),
            P(),
            P(None, None, "tp"),
            P("tp", None),
            P(),
            P("req", None, None, "tp"),
            P("req", "tp", None),
            P("req", None, None, "tp"),
            P("req", None, None),
            P("req", None, None, "tp"),
            P("req", "tp", None),
            P("req", None, None),
        ),
        out_specs=(P("req", None), P("req", None, None, "tp")),
        check_vma=False,
    )
```
